32 devices in a mesh: groups: 2 (over y), dp: 4 (over z), tensor: 4 (over x, core).
Axes of the slice: x: 2, y: 2, z: 4, core: 2. Of those that a mesh axis runs over, the one named last changes fastest.
Arguments:
- hidden_in: bfloat16 [4096, 8192], P(('groups', 'dp'), 'tensor'), parts along dimension 0, may hold values from -6 to 6
- norm_gain: float32 [8192], replicated, may hold values from 0.25 to 1.75
- w_query: bfloat16 [8192, 4096], P(None, 'tensor')
- w_keyval: bfloat16 [8192, 1024], P('tensor')
- w_out: bfloat16 [4096, 8192], P('tensor'), may hold values from -0.125 to 0.125
- hyp_ids: int32 [4096], P(('groups', 'dp')), parts along dimension 0, may hold values from -1 to 20, as said below
Outputs:
- mixed: bfloat16 [4096, 8192], P(('groups', 'dp'), 'tensor'), parts along dimension 0
The draws below stay inside these ranges and needn't reach their ends.
There are 2 independent parts, one for each index of `groups`. The reference program is written for one: setup_inputs(seed, part) draws one part's arguments, and reference() takes and returns one part's arrays. A program takes and returns all parts, laid end to end along the dimension named above; an argument that names none is the same for every part. Nothing has to cross between parts.
Inputs may be any that keep to these rules, and one draw needn't show every extreme that they name: `hyp_ids`: within each block of 512 rows of one dp index the numbers start at 0 and rise by one at each new hypothesis; padding rows (-1) only end a block; some block has no padding and holds 21 hypotheses.
All inputs are finite; a program needn't handle non-finite values.
Results may differ from the reference program's by a relative error of at most 0.0055.
Values may be sent and summed in bfloat16 or wider, within the bound.
A program may use at most 128 MiB of HBM per device.

```python
import jax
import jax.numpy as jnp
from jax import lax

D = 8192
HEADS = 32
KVH = 4
HD = 128
TOK_DEV = 512
TOKENS = 2048
N_DP = 4


def key_columns(key):
    base_key = jax.random.fold_in(key, 29)
    return jax.random.normal(base_key, (D, KVH * HD), jnp.float32) * D ** (-0.5)


def draw_hidden_in(key, part):
    key = jax.random.fold_in(key, 3)
    values = jax.random.normal(key, (TOKENS, D), jnp.float32)
    values = jnp.clip(values, -6.0, 6.0)
    return values.astype(jnp.bfloat16)


def draw_w_keyval(key, part):
    key_part = key_columns(key)
    key = jax.random.fold_in(key, 13)
    value_part = jax.random.normal(key, (D, KVH * HD), jnp.float32) * D ** (-0.5)
    return jnp.concatenate([key_part, value_part], axis=1).astype(jnp.bfloat16)


def draw_w_query(key, part):
    key = jax.random.fold_in(key, 11)
    weights = jax.random.normal(key, (D, HEADS * HD), jnp.float32) * D ** (-0.5)
    return weights.astype(jnp.bfloat16)


def draw_hyp_ids(key, part):
    key = jax.random.fold_in(key, 7)
    key_shift, key_full, key_start = jax.random.split(key, 3)
    shifts = jax.random.randint(key_shift, (N_DP,), 0, 3)
    full = jax.random.randint(key_full, (), 0, N_DP)
    shifts = jnp.where(jnp.arange(N_DP) == full, 0, shifts)
    live = jnp.right_shift(jnp.full((N_DP,), TOK_DEV, jnp.int32), shifts.astype(jnp.int32))
    count = max(TOK_DEV // 24, 2)
    block_keys = jax.random.split(key_start, N_DP)
    orders = jax.vmap(lambda k: jax.random.permutation(k, TOK_DEV - 1))(block_keys)
    chosen = orders[:, :count - 1].astype(jnp.int32) + 1
    place = jnp.arange(TOK_DEV, dtype=jnp.int32)
    starts = jnp.any(place[None, None, :] == chosen[:, :, None], axis=1)
    starts = starts | (place[None, :] == 0)
    ids = jnp.cumsum(starts.astype(jnp.int32), axis=1) - 1
    ids = jnp.where(place[None, :] < live[:, None], ids, -1)
    return ids.reshape(-1).astype(jnp.int32)


def spiked(values, rng, source, target, blocks, factor):
    def block_of(position):
        return (jnp.arange(values.shape[position]) // (values.shape[position] // blocks)).reshape((-1,) + (1,) * (values.ndim - 1 - position))

    one_side = jax.random.permutation(rng, blocks)[block_of(target)]
    far = (block_of(target) + blocks // 2) % blocks
    return jnp.where((block_of(source) == one_side) | (block_of(source) == far), factor * values, values)


def block_levels(rng, extent, pieces, least, top_value):
    loudness, own = 1.0, jax.random.fold_in(rng, 6)
    for axis_at, parts in pieces:
        steps = jnp.exp(jax.random.uniform(jax.random.fold_in(own, axis_at), (parts,), jnp.float32, least / len(pieces), top_value / len(pieces)))
        loudness = loudness * jnp.repeat(steps, extent[axis_at] // parts).reshape([-1 if axis == axis_at else 1 for axis in range(len(extent))])
    return loudness


def heavy_noise(rng, dims, width, most, pieces, heavy, kind=jnp.bfloat16):
    values = width * jax.random.normal(rng, dims, jnp.float32)
    if pieces:
        values = values * block_levels(rng, dims, pieces, -0.22, 0.18)
    return jnp.clip(spiked(values, jax.random.fold_in(rng, 3), *heavy), -most, most).astype(kind)


def setup_inputs(seed: int = 0, part: int = 0) -> dict:
    streams_of = jax.random.split(jax.random.key(seed), 7)
    part_keys = jax.random.split(jax.random.fold_in(streams_of[6], part), 7)
    hidden_in = draw_hidden_in(jax.random.fold_in(jax.random.fold_in(streams_of[6], part), 71), part)
    norm_gain = jnp.clip(1.0 + 0.15 * jax.random.normal(streams_of[1], (D,), jnp.float32), 0.25, 1.75)
    w_query = draw_w_query(jax.random.fold_in(streams_of[6], 71), part)
    w_keyval = draw_w_keyval(jax.random.fold_in(streams_of[6], 71), part)
    w_out = heavy_noise(streams_of[4], (HEADS * HD, D), (HEADS * HD) ** -0.5, 0.125, ((0, 4),), (0, 1, 4, 2.0))
    hyp_ids = draw_hyp_ids(jax.random.fold_in(jax.random.fold_in(streams_of[6], part), 71), part)
    return {"hidden_in": hidden_in, "norm_gain": norm_gain, "w_query": w_query, "w_keyval": w_keyval, "w_out": w_out, "hyp_ids": hyp_ids}


def positions(ids):
    rows = ids.shape[0]
    row = jnp.arange(rows, dtype=jnp.int32)
    prev = jnp.concatenate([jnp.full((1,), -2, jnp.int32), ids[:-1]])
    start = jnp.where(ids != prev, row, jnp.zeros_like(row))
    start = lax.cummax(start, axis=0)
    return (row - start).astype(jnp.float32)

def rotate(heads, pos):
    half = heads.shape[-1] // 2
    freq = 500000.0 ** (-jnp.arange(half, dtype=jnp.float32) * 2.0 / heads.shape[-1])
    angle = pos[:, None] * freq[None, :]
    cosine = jnp.cos(angle)[:, None, :]
    sine = jnp.sin(angle)[:, None, :]
    first = heads[..., :half]
    second = heads[..., half:]
    return jnp.concatenate([first * cosine - second * sine, second * cosine + first * sine], axis=-1)

def attend(query, keys, values, ids):
    rows = ids.shape[0]
    row = jnp.arange(rows, dtype=jnp.int32)
    allowed = (ids[:, None] == ids[None, :]) & (ids[:, None] >= 0) & (row[None, :] <= row[:, None])
    scores = jnp.einsum('qhd,khd->hqk', query.astype(jnp.float32), keys.astype(jnp.float32)) / jnp.sqrt(jnp.float32(query.shape[-1]))
    scores = jnp.where(allowed[None], scores, jnp.float32(-1e+30))
    peak = lax.optimization_barrier(jnp.max(scores, axis=-1, keepdims=True))
    expo = jnp.where(allowed[None], jnp.exp(scores - peak), jnp.float32(0.0))
    total = jnp.maximum(lax.optimization_barrier(jnp.sum(expo, axis=-1, keepdims=True)), 1.0)
    probs = (expo / total).astype(jnp.bfloat16)
    context = jnp.einsum('hqk,khd->qhd', probs.astype(jnp.float32), values.astype(jnp.float32))
    return context.astype(jnp.bfloat16).reshape(rows, -1)

def reference(hidden_in, norm_gain, w_query, w_keyval, w_out, hyp_ids):
    wide = hidden_in.astype(jnp.float32)
    scale = lax.rsqrt(lax.optimization_barrier(jnp.mean(wide * wide, axis=-1)) + 1e-05)
    normed = (wide * norm_gain[None, :]).astype(jnp.bfloat16)
    query_raw = jnp.dot(normed, w_query, preferred_element_type=jnp.float32) * scale[:, None]
    keyval = jnp.dot(normed, w_keyval, preferred_element_type=jnp.float32) * scale[:, None]
    group = HEADS // KVH

    def block(items):
        query_block, keyval_block, ids = items
        pos = positions(ids)
        query = rotate(query_block.reshape(TOK_DEV, HEADS, HD), pos).astype(jnp.bfloat16)
        keys = rotate(keyval_block[:, :KVH * HD].reshape(TOK_DEV, KVH, HD), pos).astype(jnp.bfloat16)
        values = keyval_block[:, KVH * HD:].reshape(TOK_DEV, KVH, HD).astype(jnp.bfloat16)
        keys = jnp.repeat(keys, group, axis=1)
        values = jnp.repeat(values, group, axis=1)
        return attend(query, keys, values, ids)
    context = lax.map(block, (query_raw.reshape(N_DP, TOK_DEV, HEADS * HD), keyval.reshape(N_DP, TOK_DEV, 2 * KVH * HD), hyp_ids.reshape(N_DP, TOK_DEV)))
    context = context.reshape(TOKENS, HEADS * HD)
    projected = jnp.dot(context, w_out, preferred_element_type=jnp.float32)
    return (wide + projected).astype(jnp.bfloat16)
```

```python
import functools

import jax
import jax.numpy as jnp
import numpy as np
from jax import lax
from jax.experimental import pallas as pl
from jax.experimental.pallas import tpu as pltpu
from jax.sharding import PartitionSpec as P

D = 8192
HEADS = 32
KVH = 4
HD = 128
CHUNKS = 4
MESH = pl.DeviceIdType.MESH
F32 = jnp.float32
BF16 = jnp.bfloat16


def turn(v, cosine, sine):
    return v * cosine + pltpu.roll(v, HD // 2, 1) * sine


def kernel(
    hid, gain, freq, sign, ids, wq_h, wkv_h, wo_h, out,
    g, wq, wo, nrm, kvp, kvr, kxs, kxr, kbuf, vbuf, qbuf, ctx,
    a_out, b_out, x_out, a_in, b_in, x_in, acc,
    agx_s, agc_s, fwd_s, g1_r, g2_r, g3_r, kv_s, kv_r,
    a_s, b_s, x_s, a_r, b_r, x_r, l_hid, l_kv, l_wq, l_wo, l_out,
):
    rows, width = hid.shape
    R = rows // CHUNKS
    heads = wq_h.shape[1] // HD
    half = wkv_h.shape[0] // 2
    me = lax.axis_index("tensor")
    chip, core = me // 2, me % 2
    d1 = chip * 2 + (1 - core)
    d2 = (1 - chip) * 2 + core
    d3 = 3 - me
    dev = (me, d1, d2, d3)

    barrier = pltpu.get_barrier_semaphore()
    for other in (d1, d2):
        pl.semaphore_signal(barrier, inc=1, device_id={"tensor": other}, device_id_type=MESH)

    own_copy = pltpu.make_async_copy(hid, g.at[0], l_hid.at[0])
    own_copy.start()
    kv_copies = []
    for r in range(4):
        for which in range(2):
            for h in range(2):
                col = pl.multiple_of(which * (KVH * HD) + dev[r] * HD, HD)
                kv_copies.append(
                    pltpu.make_async_copy(
                        wkv_h.at[pl.ds(h * half, half), pl.ds(col, HD)],
                        wo.at[0, :, pl.ds(h * 1024 + r * 256 + which * HD, HD)],
                        l_kv.at[(r * 2 + which) * 2 + h],
                    )
                )
    for copy in kv_copies:
        copy.start()

    pl.semaphore_wait(barrier, 2)

    def rows_of(c):
        return pl.ds(pl.multiple_of(c * R, R), R)

    def remote(src, dst, send, recv, to):
        return pltpu.make_async_remote_copy(
            src_ref=src, dst_ref=dst, send_sem=send, recv_sem=recv,
            device_id={"tensor": to}, device_id_type=MESH,
        )

    def gather_x(c):
        return remote(hid.at[rows_of(c), :], g.at[2, rows_of(c), :], agx_s.at[c], g2_r.at[c], d2)

    def gather_core(c):
        return remote(hid.at[rows_of(c), :], g.at[1, rows_of(c), :], agc_s.at[c], g1_r.at[c], d1)

    def forward(c):
        return remote(
            g.at[2, rows_of(c), :], g.at[3, rows_of(c), :], fwd_s.at[c], g3_r.at[c], d1
        )

    for c in range(2):
        gather_x(c).start()
        gather_core(c).start()

    wq_copies = [
        pltpu.make_async_copy(
            wq_h.at[pl.ds(pl.multiple_of(dev[r] * width, width), width), :], wq.at[r], l_wq.at[r]
        )
        for r in range(4)
    ]
    wo_copies = [
        pltpu.make_async_copy(
            wo_h.at[:, pl.ds(pl.multiple_of(dev[r] * width, width), width)], wo.at[r], l_wo.at[r]
        )
        for r in range(4)
    ]
    for copy in wq_copies:
        copy.start()
    for r in (3, 1, 2):
        wo_copies[r].start()

    kbuf[...] = jnp.zeros_like(kbuf)
    vbuf[...] = jnp.zeros_like(vbuf)

    own_copy.wait()
    for copy in kv_copies:
        copy.wait()

    def kv_rows(c, carry):
        for j in range(width // 512):
            x = g[0, rows_of(c), j * 512 : (j + 1) * 512].astype(F32)
            gj = gain[:, pl.ds(pl.multiple_of(me * width + j * 512, 512), 512)]
            nrm[0, :, j * 512 : (j + 1) * 512] = (x * gj).astype(BF16)
        for r in (3, 1, 2, 0):
            t = jnp.dot(
                nrm[0, :, :half], wo[0, :, r * 256 : (r + 1) * 256], preferred_element_type=F32
            )
            t += jnp.dot(
                nrm[0, :, half:],
                wo[0, :, 1024 + r * 256 : 1024 + (r + 1) * 256],
                preferred_element_type=F32,
            )
            kvp[r, rows_of(c), :] = t
        return carry

    lax.fori_loop(0, CHUNKS, kv_rows, 0)
    wo_copies[0].start()
    kv_a = remote(kvp.at[3], kvr.at[1], kv_s.at[0], kv_r.at[0], d1)
    kv_b = remote(kvp.at[1], kvr.at[0], kv_s.at[1], kv_r.at[1], d1)
    kv_x = remote(kxs, kxr, kv_s.at[2], kv_r.at[2], d2)
    kv_a.start()
    kv_b.start()
    kv_a.wait_recv()
    kxs[...] = (kvp[2] + kvr[1]).astype(BF16)
    kv_x.start()

    for copy in wq_copies:
        copy.wait()

    def chunk(c, carry):
        here = rows_of(c)
        gather_x(c).wait_recv()
        forward(c).start()
        gather_x(c).wait_send()
        gather_core(c).wait_send()

        @pl.when(c + 2 < CHUNKS)
        def _():
            gather_x(c + 2).start()
            gather_core(c + 2).start()

        row = c * R + lax.broadcasted_iota(jnp.int32, (R, rows), 0)
        col = lax.broadcasted_iota(jnp.int32, (R, rows), 1)
        ids_row = jnp.broadcast_to(ids[...].astype(F32), (R, rows))
        ids_col = jnp.sum(jnp.where(row == col, ids_row, 0.0), axis=1, keepdims=True)
        same = ids_row == ids_col
        pos = jnp.sum(jnp.where(same & (col < row), 1.0, 0.0), axis=1, keepdims=True)
        angle = pos * freq[...]
        cosine = jnp.cos(angle)
        sine = jnp.sin(angle) * sign[...]
        live = ids_col >= 0.0
        bias = jnp.where(same & (col <= row), 0.0, -1e30)

        gather_core(c).wait_recv()
        forward(c).wait_recv()
        squares = jnp.zeros((R, HD), F32)
        for r in range(4):
            for j in range(width // 512):
                x = g[r, here, j * 512 : (j + 1) * 512].astype(F32)
                gj = gain[:, pl.ds(pl.multiple_of(dev[r] * width + j * 512, 512), 512)]
                nrm[r, :, j * 512 : (j + 1) * 512] = (x * gj).astype(BF16)
                xx = x * x
                for k in range(4):
                    squares += xx[:, k * HD : (k + 1) * HD]
        scale = lax.rsqrt(jnp.sum(squares, axis=1, keepdims=True) / D + 1e-05)

        def query(n, carry):
            cols = pl.ds(pl.multiple_of(n * 256, 256), 256)
            t = jnp.dot(nrm[0], wq[0, :, cols], preferred_element_type=F32)
            for r in range(1, 4):
                t += jnp.dot(nrm[r], wq[r, :, cols], preferred_element_type=F32)
            t = t * scale
            t = jnp.concatenate(
                [turn(t[:, :HD], cosine, sine), turn(t[:, HD:], cosine, sine)], axis=1
            )
            qbuf[:, cols] = t.astype(BF16)
            return carry

        lax.fori_loop(0, heads // 2, query, 0)

        @pl.when(c == 0)
        def _():
            kv_b.wait_recv()
            kv_x.wait_recv()

        kv = (kvp[0, here, :] + kvr[0, here, :] + kxr[here, :].astype(F32)) * scale
        kbuf[here, :] = turn(kv[:, :HD], cosine, sine).astype(BF16)
        vbuf[here, :] = kv[:, HD:].astype(BF16)

        def attend(h, carry):
            for one in range(2):
                cols = pl.ds(pl.multiple_of(h * 256 + one * HD, HD), HD)
                s = lax.dot_general(
                    qbuf[:, cols], kbuf[...], (((1,), (1,)), ((), ())), preferred_element_type=F32
                )
                s = s * (HD**-0.5) + bias
                e = jnp.exp(s - jnp.max(s, axis=1, keepdims=True))
                total = jnp.maximum(jnp.sum(e, axis=1, keepdims=True), 1.0)
                p = (e * jnp.where(live, 1.0 / total, 0.0)).astype(BF16)
                ctx[here, cols] = jnp.dot(p, vbuf[...], preferred_element_type=F32).astype(BF16)
            return carry

        lax.fori_loop(0, heads // 2, attend, 0)

        send_a = remote(a_out, a_in.at[c], a_s.at[0], a_r.at[c], d1)
        send_b = remote(b_out, b_in.at[c], b_s.at[0], b_r.at[c], d1)
        send_x = remote(x_out.at[c], x_in.at[c], x_s.at[c], x_r.at[c], d2)

        @pl.when(c == 0)
        def _():
            for r in (3, 1, 2):
                wo_copies[r].wait()

        @pl.when(c > 0)
        def _():
            send_a.wait_send()
            send_b.wait_send()

        def project(r, n):
            cols = pl.ds(pl.multiple_of(n * 512, 512), 512)
            return cols, jnp.dot(ctx[here, :], wo[r, :, cols], preferred_element_type=F32)

        def part_a(n, carry):
            cols, t = project(3, n)
            a_out[:, cols] = t.astype(BF16)
            return carry

        lax.fori_loop(0, width // 512, part_a, 0)
        send_a.start()

        def part_b(n, carry):
            cols, t = project(1, n)
            b_out[:, cols] = t.astype(BF16)
            return carry

        lax.fori_loop(0, width // 512, part_b, 0)
        send_b.start()
        send_a.wait_recv()

        def part_x(n, carry):
            cols, t = project(2, n)
            x_out[c, :, cols] = (t + a_in[c, :, cols].astype(F32)).astype(BF16)
            return carry

        lax.fori_loop(0, width // 512, part_x, 0)
        send_x.start()
        return carry

    lax.fori_loop(0, CHUNKS, chunk, 0)
    wo_copies[0].wait()

    def store(c):
        return pltpu.make_async_copy(g.at[0, rows_of(c), :], out.at[rows_of(c), :], l_out.at[c])

    def finish(c, carry):
        here = rows_of(c)
        remote(b_out, b_in.at[c], b_s.at[0], b_r.at[c], d1).wait_recv()

        def own(n, carry):
            cols = pl.ds(pl.multiple_of(n * 512, 512), 512)
            t = jnp.dot(ctx[here, :], wo[0, :, cols], preferred_element_type=F32)
            acc[:, cols] = t + b_in[c, :, cols].astype(F32) + g[0, here, cols].astype(F32)
            return carry

        lax.fori_loop(0, width // 512, own, 0)
        remote(x_out.at[c], x_in.at[c], x_s.at[c], x_r.at[c], d2).wait_recv()
        for j in range(width // 512):
            cols = slice(j * 512, (j + 1) * 512)
            g[0, here, cols] = (acc[:, cols] + x_in[c, :, cols].astype(F32)).astype(BF16)
        store(c).start()
        return carry

    lax.fori_loop(0, CHUNKS, finish, 0)

    kv_a.wait_send()
    kv_b.wait_send()
    kv_x.wait_send()
    remote(a_out, a_in.at[0], a_s.at[0], a_r.at[0], d1).wait_send()
    remote(b_out, b_in.at[0], b_s.at[0], b_r.at[0], d1).wait_send()
    for c in range(CHUNKS):
        forward(c).wait_send()
        remote(x_out.at[c], x_in.at[c], x_s.at[c], x_r.at[c], d2).wait_send()
        store(c).wait()


def fused(hidden_in, norm_gain, w_query, w_keyval, w_out, hyp_ids):
    rows, width = hidden_in.shape
    R = rows // CHUNKS
    qc = w_query.shape[1]
    exponent = np.arange(HD // 2, dtype=np.float32) * np.float32(2.0 / HD)
    base = np.power(np.float32(500000.0), -exponent).astype(np.float32)
    freq = jnp.asarray(np.concatenate([base, base])[None, :])
    sign = jnp.asarray(np.repeat(np.float32([-1.0, 1.0]), HD // 2)[None, :])
    vmem = pl.BlockSpec(memory_space=pltpu.VMEM)
    hbm = pl.BlockSpec(memory_space=pl.ANY)
    dma = pltpu.SemaphoreType.DMA
    return pl.pallas_call(
        kernel,
        out_shape=jax.ShapeDtypeStruct((rows, width), BF16),
        in_specs=[hbm, vmem, vmem, vmem, vmem, hbm, hbm, hbm],
        out_specs=hbm,
        scratch_shapes=[
            pltpu.VMEM((4, rows, width), BF16),
            pltpu.VMEM((4, width, qc), BF16),
            pltpu.VMEM((4, qc, width), BF16),
            pltpu.VMEM((4, R, width), BF16),
            pltpu.VMEM((4, rows, 2 * HD), F32),
            pltpu.VMEM((2, rows, 2 * HD), F32),
            pltpu.VMEM((rows, 2 * HD), BF16),
            pltpu.VMEM((rows, 2 * HD), BF16),
            pltpu.VMEM((rows, HD), BF16),
            pltpu.VMEM((rows, HD), BF16),
            pltpu.VMEM((R, qc), BF16),
            pltpu.VMEM((rows, qc), BF16),
            pltpu.VMEM((R, width), BF16),
            pltpu.VMEM((R, width), BF16),
            pltpu.VMEM((CHUNKS, R, width), BF16),
            pltpu.VMEM((CHUNKS, R, width), BF16),
            pltpu.VMEM((CHUNKS, R, width), BF16),
            pltpu.VMEM((CHUNKS, R, width), BF16),
            pltpu.VMEM((R, width), F32),
            dma((CHUNKS,)), dma((CHUNKS,)), dma((CHUNKS,)),
            dma((CHUNKS,)), dma((CHUNKS,)), dma((CHUNKS,)),
            dma((3,)), dma((3,)),
            dma((1,)), dma((1,)), dma((CHUNKS,)),
            dma((CHUNKS,)), dma((CHUNKS,)), dma((CHUNKS,)),
            dma((1,)), dma((16,)), dma((4,)), dma((4,)), dma((CHUNKS,)),
        ],
        compiler_params=pltpu.CompilerParams(
            collective_id=0, has_side_effects=True, vmem_limit_bytes=VMEM_LIMIT
        ),
    )(
        hidden_in, norm_gain.reshape(1, -1), freq, sign, hyp_ids.reshape(1, -1),
        w_query, w_keyval, w_out,
    )


VMEM_LIMIT = 62 * 1024 * 1024


def positions(ids):
    rows = ids.shape[0]
    row = jnp.arange(rows, dtype=jnp.int32)
    prev = jnp.concatenate([jnp.full((1,), -2, jnp.int32), ids[:-1]])
    start = jnp.where(ids != prev, row, jnp.zeros_like(row))
    start = lax.cummax(start, axis=0)
    return (row - start).astype(jnp.float32)


def rotate(heads, pos):
    half = heads.shape[-1] // 2
    freq = 500000.0 ** (-jnp.arange(half, dtype=jnp.float32) * 2.0 / heads.shape[-1])
    angle = pos[:, None] * freq[None, :]
    cosine = jnp.cos(angle)[:, None, :]
    sine = jnp.sin(angle)[:, None, :]
    first = heads[..., :half]
    second = heads[..., half:]
    return jnp.concatenate(
        [first * cosine - second * sine, second * cosine + first * sine], axis=-1
    )


def shards(hidden_in, norm_gain, w_query, w_keyval, w_out, hyp_ids):
    rows = hidden_in.shape[0]
    local_width = hidden_in.shape[1]
    shard = lax.axis_index("tensor")
    local_gain = lax.dynamic_slice_in_dim(norm_gain, shard * local_width, local_width)
    local_normed = (hidden_in.astype(jnp.float32) * local_gain[None, :]).astype(jnp.bfloat16)
    kv_term = jnp.dot(local_normed, w_keyval, preferred_element_type=jnp.float32)
    keyval = lax.psum(kv_term, "tensor")
    whole = lax.all_gather(hidden_in, "tensor", axis=1, tiled=True)
    wide = whole.astype(jnp.float32)
    squares = jnp.sum(wide * wide, axis=-1)
    normed = (wide * norm_gain[None, :]).astype(jnp.bfloat16)
    query_raw = jnp.dot(normed, w_query, preferred_element_type=jnp.float32)
    scale = lax.rsqrt(squares / D + 1e-05)
    pos = positions(hyp_ids)
    local_heads = w_query.shape[1] // HD
    query = rotate((query_raw * scale[:, None]).reshape(rows, local_heads, HD), pos).astype(
        jnp.bfloat16
    )
    keyval = keyval * scale[:, None]
    keys = rotate(keyval[:, : KVH * HD].reshape(rows, KVH, HD), pos)
    values = keyval[:, KVH * HD :].reshape(rows, KVH, HD)
    group = HEADS // KVH
    head_index = shard * local_heads + jnp.arange(local_heads, dtype=jnp.int32)
    select = (head_index[:, None] // group == jnp.arange(KVH, dtype=jnp.int32)[None, :]).astype(
        jnp.float32
    )
    keys = jnp.einsum("tgd,hg->thd", keys.astype(jnp.bfloat16).astype(jnp.float32), select).astype(
        jnp.bfloat16
    )
    values = jnp.einsum(
        "tgd,hg->thd", values.astype(jnp.bfloat16).astype(jnp.float32), select
    ).astype(jnp.bfloat16)
    row = jnp.arange(rows, dtype=jnp.int32)
    allowed = (
        (hyp_ids[:, None] == hyp_ids[None, :])
        & (hyp_ids[:, None] >= 0)
        & (row[None, :] <= row[:, None])
    )
    scores = jnp.einsum("qhd,khd->hqk", query, keys, preferred_element_type=jnp.float32) / jnp.sqrt(
        jnp.float32(HD)
    )
    scores = jnp.where(allowed[None], scores, jnp.float32(-1e30))
    peak = jnp.max(scores, axis=-1, keepdims=True)
    expo = jnp.where(allowed[None], jnp.exp(scores - peak), jnp.float32(0.0))
    total = jnp.maximum(jnp.sum(expo, axis=-1, keepdims=True), 1.0)
    probs = (expo / total).astype(jnp.bfloat16)
    context = jnp.einsum("hqk,khd->qhd", probs, values, preferred_element_type=jnp.float32)
    context = context.astype(jnp.bfloat16).reshape(rows, local_heads * HD)
    out_term = jnp.dot(context, w_out, preferred_element_type=jnp.float32)
    summed = lax.psum_scatter(out_term, "tensor", scatter_dimension=1, tiled=True)
    return (hidden_in.astype(jnp.float32) + summed).astype(jnp.bfloat16)


def solution(mesh):
    body = fused if mesh.shape["tensor"] == 4 else shards
    return jax.shard_map(
        body,
        mesh=mesh,
        in_specs=(
            P(("groups", "dp"), "tensor"),
            P(),
            P(None, "tensor"),
            P("tensor", None),
            P("tensor", None),
            P(("groups", "dp")),
        ),
        out_specs=P(("groups", "dp"), "tensor"),
        check_vma=False,
    )
```

```python
import functools

import jax
import jax.numpy as jnp
import numpy as np
from jax import lax
from jax.experimental import pallas as pl
from jax.experimental.pallas import tpu as pltpu
from jax.sharding import PartitionSpec as P

D = 8192
HEADS = 32
KVH = 4
HD = 128
CHUNKS = 4
MESH = pl.DeviceIdType.MESH
F32 = jnp.float32
BF16 = jnp.bfloat16


def turn(v, cosine, sine):
    return v * cosine + pltpu.roll(v, HD // 2, 1) * sine


def kernel(
    hid, gain, freq, sign, ids, wq_h, wkv_h, wo_h, out,
    far, wq, wo, nrm, kvp, kvr, kxs, kxr, kbuf, vbuf, qbuf, ctx,
    a_out, b_out, x_out, a_in, b_in, x_in,
    agx_s, agc_s, fwd_s, g1_r, g2_r, g3_r, kv_s, kv_r,
    a_s, b_s, x_s, a_r, b_r, x_r, l_hid, l_kv, l_wq, l_wo,
):
    rows, width = hid.shape
    R = rows // CHUNKS
    heads = wq_h.shape[1] // HD
    half = wkv_h.shape[0] // 2
    me = lax.axis_index("tensor")
    chip, core = me // 2, me % 2
    d1 = chip * 2 + (1 - core)
    d2 = (1 - chip) * 2 + core
    d3 = 3 - me
    dev = (me, d1, d2, d3)
    g = (out, far.at[0], far.at[1], far.at[2])

    barrier = pltpu.get_barrier_semaphore()
    for other in (d1, d2):
        pl.semaphore_signal(barrier, inc=1, device_id={"tensor": other}, device_id_type=MESH)

    own_copy = pltpu.make_async_copy(hid, out, l_hid.at[0])
    kv_copies = []
    for r in range(4):
        for which in range(2):
            for h in range(2):
                col = pl.multiple_of(which * (KVH * HD) + dev[r] * HD, HD)
                kv_copies.append(
                    pltpu.make_async_copy(
                        wkv_h.at[pl.ds(h * half, half), pl.ds(col, HD)],
                        wo.at[0, :, pl.ds(h * 1024 + r * 256 + which * HD, HD)],
                        l_kv.at[(r * 2 + which) * 2 + h],
                    )
                )

    def rows_of(c):
        return pl.ds(pl.multiple_of(c * R, R), R)

    def remote(src, dst, send, recv, to):
        return pltpu.make_async_remote_copy(
            src_ref=src, dst_ref=dst, send_sem=send, recv_sem=recv,
            device_id={"tensor": to}, device_id_type=MESH,
        )

    def gather_x(c):
        return remote(hid.at[rows_of(c), :], far.at[1, rows_of(c), :], agx_s.at[c], g2_r.at[c], d2)

    def gather_core(c):
        return remote(hid.at[rows_of(c), :], far.at[0, rows_of(c), :], agc_s.at[c], g1_r.at[c], d1)

    def forward(c):
        return remote(
            far.at[1, rows_of(c), :], far.at[2, rows_of(c), :], fwd_s.at[c], g3_r.at[c], d1
        )

    pl.semaphore_wait(barrier, 2)
    gather_x(0).start()
    own_copy.start()
    for copy in kv_copies:
        copy.start()
    for c in range(CHUNKS):
        gather_core(c).start()

    wq_copies = [
        pltpu.make_async_copy(
            wq_h.at[pl.ds(pl.multiple_of(dev[r] * width, width), width), :], wq.at[r], l_wq.at[r]
        )
        for r in range(4)
    ]
    wo_copies = [
        pltpu.make_async_copy(
            wo_h.at[:, pl.ds(pl.multiple_of(dev[r] * width, width), width)], wo.at[r], l_wo.at[r]
        )
        for r in range(4)
    ]
    kbuf[...] = jnp.zeros_like(kbuf)
    vbuf[...] = jnp.zeros_like(vbuf)

    own_copy.wait()
    for copy in kv_copies:
        copy.wait()
    for copy in wq_copies:
        copy.start()

    def kv_rows(c, carry):
        for j in range(width // 512):
            x = out[rows_of(c), j * 512 : (j + 1) * 512].astype(F32)
            gj = gain[:, pl.ds(pl.multiple_of(me * width + j * 512, 512), 512)]
            nrm[0, :, j * 512 : (j + 1) * 512] = (x * gj).astype(BF16)
        for r in (3, 1, 2, 0):
            t = jnp.dot(
                nrm[0, :, :half], wo[0, :, r * 256 : (r + 1) * 256], preferred_element_type=F32
            )
            t += jnp.dot(
                nrm[0, :, half:],
                wo[0, :, 1024 + r * 256 : 1024 + (r + 1) * 256],
                preferred_element_type=F32,
            )
            kvp[r, rows_of(c), :] = t
        return carry

    lax.fori_loop(0, CHUNKS, kv_rows, 0)
    kv_a = remote(kvp.at[3], kvr.at[1], kv_s.at[0], kv_r.at[0], d1)
    kv_b = remote(kvp.at[1], kvr.at[0], kv_s.at[1], kv_r.at[1], d1)
    kv_x = remote(kxs, kxr, kv_s.at[2], kv_r.at[2], d2)
    kv_a.start()
    kv_b.start()
    gather_x(1).start()
    for r in (3, 1, 2, 0):
        wo_copies[r].start()
    kv_a.wait_recv()
    kxs[...] = (kvp[2] + kvr[1]).astype(BF16)
    kv_x.start()

    for copy in wq_copies:
        copy.wait()

    def chunk(c, carry):
        here = rows_of(c)
        gather_x(c).wait_recv()
        forward(c).start()

        row = c * R + lax.broadcasted_iota(jnp.int32, (R, rows), 0)
        col = lax.broadcasted_iota(jnp.int32, (R, rows), 1)
        ids_row = jnp.broadcast_to(ids[...].astype(F32), (R, rows))
        ids_col = jnp.sum(jnp.where(row == col, ids_row, 0.0), axis=1, keepdims=True)
        same = ids_row == ids_col
        pos = jnp.sum(jnp.where(same & (col < row), 1.0, 0.0), axis=1, keepdims=True)
        angle = pos * freq[...]
        cosine = jnp.cos(angle)
        sine = jnp.sin(angle) * sign[...]
        live = ids_col >= 0.0
        bias = jnp.where(same & (col <= row), 0.0, -1e30)

        gather_core(c).wait_recv()
        forward(c).wait_recv()
        squares = jnp.zeros((R, HD), F32)
        for r in range(4):
            for j in range(width // 512):
                x = g[r][here, j * 512 : (j + 1) * 512].astype(F32)
                gj = gain[:, pl.ds(pl.multiple_of(dev[r] * width + j * 512, 512), 512)]
                nrm[r, :, j * 512 : (j + 1) * 512] = (x * gj).astype(BF16)
                xx = x * x
                for k in range(4):
                    squares += xx[:, k * HD : (k + 1) * HD]
        scale = lax.rsqrt(jnp.sum(squares, axis=1, keepdims=True) / D + 1e-05)

        def query(n, carry):
            cols = pl.ds(pl.multiple_of(n * 256, 256), 256)
            t = jnp.dot(nrm[0], wq[0, :, cols], preferred_element_type=F32)
            for r in range(1, 4):
                t += jnp.dot(nrm[r], wq[r, :, cols], preferred_element_type=F32)
            t = t * scale
            t = jnp.concatenate(
                [turn(t[:, :HD], cosine, sine), turn(t[:, HD:], cosine, sine)], axis=1
            )
            qbuf[:, cols] = t.astype(BF16)
            return carry

        lax.fori_loop(0, heads // 2, query, 0)

        @pl.when(c + 2 < CHUNKS)
        def _():
            gather_x(c + 2).start()

        @pl.when(c == 0)
        def _():
            kv_b.wait_recv()
            kv_x.wait_recv()

        kv = (kvp[0, here, :] + kvr[0, here, :] + kxr[here, :].astype(F32)) * scale
        kbuf[here, :] = turn(kv[:, :HD], cosine, sine).astype(BF16)
        vbuf[here, :] = kv[:, HD:].astype(BF16)

        for upto in range(CHUNKS):
            keys = (upto + 1) * R

            def attend(h, carry, keys=keys):
                for one in range(2):
                    cols = pl.ds(pl.multiple_of(h * 256 + one * HD, HD), HD)
                    s = lax.dot_general(
                        qbuf[:, cols], kbuf[:keys, :], (((1,), (1,)), ((), ())),
                        preferred_element_type=F32,
                    )
                    s = s * (HD**-0.5) + bias[:, :keys]
                    e = jnp.exp(s - jnp.max(s, axis=1, keepdims=True))
                    total = jnp.maximum(jnp.sum(e, axis=1, keepdims=True), 1.0)
                    p = (e * jnp.where(live, 1.0 / total, 0.0)).astype(BF16)
                    t = jnp.dot(p, vbuf[:keys, :], preferred_element_type=F32)
                    ctx[here, cols] = t.astype(BF16)
                return carry

            @pl.when(c == upto)
            def _(attend=attend):
                lax.fori_loop(0, heads // 2, attend, 0)

        send_a = remote(a_out, a_in.at[c], a_s.at[0], a_r.at[c], d1)
        send_b = remote(b_out, b_in.at[c], b_s.at[0], b_r.at[c], d1)
        send_x = remote(x_out.at[c], x_in.at[c], x_s.at[c], x_r.at[c], d2)

        @pl.when(c == 0)
        def _():
            for r in (3, 1, 2):
                wo_copies[r].wait()

        @pl.when(c > 0)
        def _():
            send_a.wait_send()
            send_b.wait_send()

        def project(r, n):
            cols = pl.ds(pl.multiple_of(n * 512, 512), 512)
            return cols, jnp.dot(ctx[here, :], wo[r, :, cols], preferred_element_type=F32)

        def part_a(n, carry):
            cols, t = project(3, n)
            a_out[:, cols] = t.astype(BF16)
            return carry

        lax.fori_loop(0, width // 512, part_a, 0)
        send_a.start()

        def part_b(n, carry):
            cols, t = project(1, n)
            b_out[:, cols] = t.astype(BF16)
            return carry

        lax.fori_loop(0, width // 512, part_b, 0)
        send_b.start()
        send_a.wait_recv()

        def part_x(n, carry):
            cols, t = project(2, n)
            x_out[c, :, cols] = (t + a_in[c, :, cols].astype(F32)).astype(BF16)
            return carry

        lax.fori_loop(0, width // 512, part_x, 0)
        send_x.start()
        return carry

    lax.fori_loop(0, CHUNKS, chunk, 0)
    wo_copies[0].wait()

    def prepare(c):
        remote(b_out, b_in.at[c], b_s.at[0], b_r.at[c], d1).wait_recv()

        def own(n, carry):
            cols = pl.ds(pl.multiple_of(n * 256, 256), 256)
            t = jnp.dot(ctx[rows_of(c), :], wo[0, :, cols], preferred_element_type=F32)
            t = t + b_in[c, :, cols].astype(F32) + out[rows_of(c), cols].astype(F32)
            kvp[(c % 2) * 2 + n // 4, pl.ds(pl.multiple_of((n % 4) * R, R), R), :] = t
            return carry

        lax.fori_loop(0, width // 256, own, 0)

    kv_a.wait_send()
    kv_b.wait_send()
    prepare(0)

    def finish(c, carry):
        @pl.when(c + 1 < CHUNKS)
        def _():
            prepare(c + 1)

        remote(x_out.at[c], x_in.at[c], x_s.at[c], x_r.at[c], d2).wait_recv()
        for n in range(width // 256):
            cols = slice(n * 256, (n + 1) * 256)
            t = kvp[(c % 2) * 2 + n // 4, (n % 4) * R : (n % 4 + 1) * R, :]
            out[rows_of(c), cols] = (t + x_in[c, :, cols].astype(F32)).astype(BF16)
        return carry

    lax.fori_loop(0, CHUNKS, finish, 0)

    kv_x.wait_send()
    remote(a_out, a_in.at[0], a_s.at[0], a_r.at[0], d1).wait_send()
    remote(b_out, b_in.at[0], b_s.at[0], b_r.at[0], d1).wait_send()
    for c in range(CHUNKS):
        gather_x(c).wait_send()
        gather_core(c).wait_send()
        forward(c).wait_send()
        remote(x_out.at[c], x_in.at[c], x_s.at[c], x_r.at[c], d2).wait_send()


def fused(hidden_in, norm_gain, w_query, w_keyval, w_out, hyp_ids):
    rows, width = hidden_in.shape
    R = rows // CHUNKS
    qc = w_query.shape[1]
    exponent = np.arange(HD // 2, dtype=np.float32) * np.float32(2.0 / HD)
    base = np.power(np.float32(500000.0), -exponent).astype(np.float32)
    freq = jnp.asarray(np.concatenate([base, base])[None, :])
    sign = jnp.asarray(np.repeat(np.float32([-1.0, 1.0]), HD // 2)[None, :])
    vmem = pl.BlockSpec(memory_space=pltpu.VMEM)
    hbm = pl.BlockSpec(memory_space=pl.ANY)
    dma = pltpu.SemaphoreType.DMA
    return pl.pallas_call(
        kernel,
        out_shape=pltpu.VMEM((rows, width), BF16),
        in_specs=[hbm, vmem, vmem, vmem, vmem, hbm, hbm, hbm],
        out_specs=vmem,
        scratch_shapes=[
            pltpu.VMEM((3, rows, width), BF16),
            pltpu.VMEM((4, width, qc), BF16),
            pltpu.VMEM((4, qc, width), BF16),
            pltpu.VMEM((4, R, width), BF16),
            pltpu.VMEM((4, rows, 2 * HD), F32),
            pltpu.VMEM((2, rows, 2 * HD), F32),
            pltpu.VMEM((rows, 2 * HD), BF16),
            pltpu.VMEM((rows, 2 * HD), BF16),
            pltpu.VMEM((rows, HD), BF16),
            pltpu.VMEM((rows, HD), BF16),
            pltpu.VMEM((R, qc), BF16),
            pltpu.VMEM((rows, qc), BF16),
            pltpu.VMEM((R, width), BF16),
            pltpu.VMEM((R, width), BF16),
            pltpu.VMEM((CHUNKS, R, width), BF16),
            pltpu.VMEM((CHUNKS, R, width), BF16),
            pltpu.VMEM((CHUNKS, R, width), BF16),
            pltpu.VMEM((CHUNKS, R, width), BF16),
            dma((CHUNKS,)), dma((CHUNKS,)), dma((CHUNKS,)),
            dma((CHUNKS,)), dma((CHUNKS,)), dma((CHUNKS,)),
            dma((3,)), dma((3,)),
            dma((1,)), dma((1,)), dma((CHUNKS,)),
            dma((CHUNKS,)), dma((CHUNKS,)), dma((CHUNKS,)),
            dma((1,)), dma((16,)), dma((4,)), dma((4,)),
        ],
        compiler_params=pltpu.CompilerParams(
            collective_id=0, has_side_effects=True, vmem_limit_bytes=VMEM_LIMIT
        ),
    )(
        hidden_in, norm_gain.reshape(1, -1), freq, sign, hyp_ids.reshape(1, -1),
        w_query, w_keyval, w_out,
    )


VMEM_LIMIT = 60 * 1024 * 1024


def positions(ids):
    rows = ids.shape[0]
    row = jnp.arange(rows, dtype=jnp.int32)
    prev = jnp.concatenate([jnp.full((1,), -2, jnp.int32), ids[:-1]])
    start = jnp.where(ids != prev, row, jnp.zeros_like(row))
    start = lax.cummax(start, axis=0)
    return (row - start).astype(jnp.float32)


def rotate(heads, pos):
    half = heads.shape[-1] // 2
    freq = 500000.0 ** (-jnp.arange(half, dtype=jnp.float32) * 2.0 / heads.shape[-1])
    angle = pos[:, None] * freq[None, :]
    cosine = jnp.cos(angle)[:, None, :]
    sine = jnp.sin(angle)[:, None, :]
    first = heads[..., :half]
    second = heads[..., half:]
    return jnp.concatenate(
        [first * cosine - second * sine, second * cosine + first * sine], axis=-1
    )


def shards(hidden_in, norm_gain, w_query, w_keyval, w_out, hyp_ids):
    rows = hidden_in.shape[0]
    local_width = hidden_in.shape[1]
    shard = lax.axis_index("tensor")
    local_gain = lax.dynamic_slice_in_dim(norm_gain, shard * local_width, local_width)
    local_normed = (hidden_in.astype(jnp.float32) * local_gain[None, :]).astype(jnp.bfloat16)
    kv_term = jnp.dot(local_normed, w_keyval, preferred_element_type=jnp.float32)
    keyval = lax.psum(kv_term, "tensor")
    whole = lax.all_gather(hidden_in, "tensor", axis=1, tiled=True)
    wide = whole.astype(jnp.float32)
    squares = jnp.sum(wide * wide, axis=-1)
    normed = (wide * norm_gain[None, :]).astype(jnp.bfloat16)
    query_raw = jnp.dot(normed, w_query, preferred_element_type=jnp.float32)
    scale = lax.rsqrt(squares / D + 1e-05)
    pos = positions(hyp_ids)
    local_heads = w_query.shape[1] // HD
    query = rotate((query_raw * scale[:, None]).reshape(rows, local_heads, HD), pos).astype(
        jnp.bfloat16
    )
    keyval = keyval * scale[:, None]
    keys = rotate(keyval[:, : KVH * HD].reshape(rows, KVH, HD), pos)
    values = keyval[:, KVH * HD :].reshape(rows, KVH, HD)
    group = HEADS // KVH
    head_index = shard * local_heads + jnp.arange(local_heads, dtype=jnp.int32)
    select = (head_index[:, None] // group == jnp.arange(KVH, dtype=jnp.int32)[None, :]).astype(
        jnp.float32
    )
    keys = jnp.einsum("tgd,hg->thd", keys.astype(jnp.bfloat16).astype(jnp.float32), select).astype(
        jnp.bfloat16
    )
    values = jnp.einsum(
        "tgd,hg->thd", values.astype(jnp.bfloat16).astype(jnp.float32), select
    ).astype(jnp.bfloat16)
    row = jnp.arange(rows, dtype=jnp.int32)
    allowed = (
        (hyp_ids[:, None] == hyp_ids[None, :])
        & (hyp_ids[:, None] >= 0)
        & (row[None, :] <= row[:, None])
    )
    scores = jnp.einsum("qhd,khd->hqk", query, keys, preferred_element_type=jnp.float32) / jnp.sqrt(
        jnp.float32(HD)
    )
    scores = jnp.where(allowed[None], scores, jnp.float32(-1e30))
    peak = jnp.max(scores, axis=-1, keepdims=True)
    expo = jnp.where(allowed[None], jnp.exp(scores - peak), jnp.float32(0.0))
    total = jnp.maximum(jnp.sum(expo, axis=-1, keepdims=True), 1.0)
    probs = (expo / total).astype(jnp.bfloat16)
    context = jnp.einsum("hqk,khd->qhd", probs, values, preferred_element_type=jnp.float32)
    context = context.astype(jnp.bfloat16).reshape(rows, local_heads * HD)
    out_term = jnp.dot(context, w_out, preferred_element_type=jnp.float32)
    summed = lax.psum_scatter(out_term, "tensor", scatter_dimension=1, tiled=True)
    return (hidden_in.astype(jnp.float32) + summed).astype(jnp.bfloat16)


def solution(mesh):
    body = fused if mesh.shape["tensor"] == 4 else shards
    return jax.shard_map(
        body,
        mesh=mesh,
        in_specs=(
            P(("groups", "dp"), "tensor"),
            P(),
            P(None, "tensor"),
            P("tensor", None),
            P("tensor", None),
            P(("groups", "dp")),
        ),
        out_specs=P(("groups", "dp"), "tensor"),
        check_vma=False,
    )
```

```python
import functools

import jax
import jax.numpy as jnp
import numpy as np
from jax import lax
from jax.experimental import pallas as pl
from jax.experimental.pallas import tpu as pltpu
from jax.sharding import PartitionSpec as P

D = 8192
HEADS = 32
KVH = 4
HD = 128
CHUNKS = 4
MESH = pl.DeviceIdType.MESH
F32 = jnp.float32
BF16 = jnp.bfloat16


def turn(v, cosine, sine):
    return v * cosine + pltpu.roll(v, HD // 2, 1) * sine


def kernel(
    hid, gain_h, freq_h, ids_h, wq_h, wkv_h, wo_h, out,
    gain, freq, ids,    far, wq, wo, nrm, kvp, kvr, kxs, kxr, kbuf, vbuf, qbuf, ctx,
    a_out, b_out, x_out, a_in, b_in, x_in,
    agx_s, agc_s, fwd_s, g1_r, g2_r, g3_r, kv_s, kv_r,
    a_s, b_s, x_s, a_r, b_r, x_r, l_small, l_hid, l_kv, l_wq, l_wo,
):
    rows, width = hid.shape
    R = rows // CHUNKS
    heads = wq_h.shape[1] // HD
    half = wkv_h.shape[0] // 2
    me = lax.axis_index("tensor")
    chip, core = me // 2, me % 2
    d1 = chip * 2 + (1 - core)
    d2 = (1 - chip) * 2 + core
    d3 = 3 - me
    dev = (me, d1, d2, d3)
    g = (out, far.at[0], far.at[1], far.at[2])

    barrier = pltpu.get_barrier_semaphore()
    for other in (d1, d2):
        pl.semaphore_signal(barrier, inc=1, device_id={"tensor": other}, device_id_type=MESH)

    own_copy = pltpu.make_async_copy(hid, out, l_hid.at[0])
    kv_copies = []
    for r in range(4):
        for which in range(2):
            for h in range(2):
                col = pl.multiple_of(which * (KVH * HD) + dev[r] * HD, HD)
                kv_copies.append(
                    pltpu.make_async_copy(
                        wkv_h.at[pl.ds(h * half, half), pl.ds(col, HD)],
                        wo.at[0, :, pl.ds(h * 1024 + r * 256 + which * HD, HD)],
                        l_kv.at[(r * 2 + which) * 2 + h],
                    )
                )

    def rows_of(c):
        return pl.ds(pl.multiple_of(c * R, R), R)

    def remote(src, dst, send, recv, to):
        return pltpu.make_async_remote_copy(
            src_ref=src, dst_ref=dst, send_sem=send, recv_sem=recv,
            device_id={"tensor": to}, device_id_type=MESH,
        )

    def gather_x(c):
        return remote(hid.at[rows_of(c), :], far.at[1, rows_of(c), :], agx_s.at[c], g2_r.at[c], d2)

    def gather_core(c):
        return remote(hid.at[rows_of(c), :], far.at[0, rows_of(c), :], agc_s.at[c], g1_r.at[c], d1)

    def forward(c):
        return remote(
            far.at[1, rows_of(c), :], far.at[2, rows_of(c), :], fwd_s.at[c], g3_r.at[c], d1
        )

    pl.semaphore_wait(barrier, 2)
    gather_x(0).start()
    own_copy.start()
    small = [
        pltpu.make_async_copy(src, dst, l_small.at[i])
        for i, (src, dst) in enumerate(((gain_h, gain), (freq_h, freq), (ids_h, ids)))
    ]
    for copy in small:
        copy.start()
    for copy in kv_copies:
        copy.start()
    for c in range(CHUNKS):
        gather_core(c).start()

    wq_copies = [
        pltpu.make_async_copy(
            wq_h.at[pl.ds(pl.multiple_of(dev[r] * width, width), width), :], wq.at[r], l_wq.at[r]
        )
        for r in range(4)
    ]
    wo_copies = [
        pltpu.make_async_copy(
            wo_h.at[:, pl.ds(pl.multiple_of(dev[r] * width, width), width)], wo.at[r], l_wo.at[r]
        )
        for r in range(4)
    ]
    kbuf[...] = jnp.zeros_like(kbuf)
    vbuf[...] = jnp.zeros_like(vbuf)

    own_copy.wait()
    for copy in small:
        copy.wait()
    for copy in kv_copies:
        copy.wait()
    for copy in wq_copies:
        copy.start()

    def kv_rows(c, carry):
        for j in range(width // 512):
            x = out[rows_of(c), j * 512 : (j + 1) * 512].astype(F32)
            gj = gain[:, pl.ds(pl.multiple_of(me * width + j * 512, 512), 512)]
            nrm[0, :, j * 512 : (j + 1) * 512] = (x * gj).astype(BF16)
        for r in (3, 1, 2, 0):
            t = jnp.dot(
                nrm[0, :, :half], wo[0, :, r * 256 : (r + 1) * 256], preferred_element_type=F32
            )
            t += jnp.dot(
                nrm[0, :, half:],
                wo[0, :, 1024 + r * 256 : 1024 + (r + 1) * 256],
                preferred_element_type=F32,
            )
            kvp[r, rows_of(c), :] = t
        return carry

    lax.fori_loop(0, CHUNKS, kv_rows, 0)
    kv_a = remote(kvp.at[3], kvr.at[1], kv_s.at[0], kv_r.at[0], d1)
    kv_b = remote(kvp.at[1], kvr.at[0], kv_s.at[1], kv_r.at[1], d1)
    kv_x = remote(kxs, kxr, kv_s.at[2], kv_r.at[2], d2)
    kv_a.start()
    kv_b.start()
    gather_x(1).start()
    for r in (3, 1, 2, 0):
        wo_copies[r].start()
    kv_a.wait_recv()
    kxs[...] = (kvp[2] + kvr[1]).astype(BF16)
    kv_x.start()

    for copy in wq_copies:
        copy.wait()

    def chunk(c, carry):
        here = rows_of(c)
        gather_x(c).wait_recv()
        forward(c).start()

        row = c * R + lax.broadcasted_iota(jnp.int32, (R, rows), 0)
        col = lax.broadcasted_iota(jnp.int32, (R, rows), 1)
        ids_row = jnp.broadcast_to(ids[...].astype(F32), (R, rows))
        ids_col = jnp.sum(jnp.where(row == col, ids_row, 0.0), axis=1, keepdims=True)
        same = ids_row == ids_col
        pos = jnp.sum(jnp.where(same & (col < row), 1.0, 0.0), axis=1, keepdims=True)
        angle = pos * freq[...]
        cosine = jnp.cos(angle)
        sine = jnp.sin(angle)
        lane = lax.broadcasted_iota(jnp.int32, (R, HD), 1)
        sine = jnp.where(lane < HD // 2, -sine, sine)
        live = ids_col >= 0.0
        bias = jnp.where(same & (col <= row), 0.0, -1e30)

        gather_core(c).wait_recv()
        forward(c).wait_recv()
        squares = jnp.zeros((R, HD), F32)
        for r in range(4):
            for j in range(width // 512):
                x = g[r][here, j * 512 : (j + 1) * 512].astype(F32)
                gj = gain[:, pl.ds(pl.multiple_of(dev[r] * width + j * 512, 512), 512)]
                nrm[r, :, j * 512 : (j + 1) * 512] = (x * gj).astype(BF16)
                xx = x * x
                for k in range(4):
                    squares += xx[:, k * HD : (k + 1) * HD]
        scale = lax.rsqrt(jnp.sum(squares, axis=1, keepdims=True) / D + 1e-05)

        def query(n, carry):
            cols = pl.ds(pl.multiple_of(n * 256, 256), 256)
            t = jnp.dot(nrm[0], wq[0, :, cols], preferred_element_type=F32)
            for r in range(1, 4):
                t += jnp.dot(nrm[r], wq[r, :, cols], preferred_element_type=F32)
            t = t * scale
            t = jnp.concatenate(
                [turn(t[:, :HD], cosine, sine), turn(t[:, HD:], cosine, sine)], axis=1
            )
            qbuf[:, cols] = t.astype(BF16)
            return carry

        lax.fori_loop(0, heads // 2, query, 0)

        @pl.when(c + 2 < CHUNKS)
        def _():
            gather_x(c + 2).start()

        @pl.when(c == 0)
        def _():
            kv_b.wait_recv()
            kv_x.wait_recv()

        kv = (kvp[0, here, :] + kvr[0, here, :] + kxr[here, :].astype(F32)) * scale
        kbuf[here, :] = turn(kv[:, :HD], cosine, sine).astype(BF16)
        vbuf[here, :] = kv[:, HD:].astype(BF16)

        for upto in range(CHUNKS):
            keys = (upto + 1) * R

            def attend(h, carry, keys=keys):
                for one in range(2):
                    cols = pl.ds(pl.multiple_of(h * 256 + one * HD, HD), HD)
                    s = lax.dot_general(
                        qbuf[:, cols], kbuf[:keys, :], (((1,), (1,)), ((), ())),
                        preferred_element_type=F32,
                    )
                    s = s * (HD**-0.5) + bias[:, :keys]
                    e = jnp.exp(s - jnp.max(s, axis=1, keepdims=True))
                    total = jnp.maximum(jnp.sum(e, axis=1, keepdims=True), 1.0)
                    p = (e * jnp.where(live, 1.0 / total, 0.0)).astype(BF16)
                    t = jnp.dot(p, vbuf[:keys, :], preferred_element_type=F32)
                    ctx[here, cols] = t.astype(BF16)
                return carry

            @pl.when(c == upto)
            def _(attend=attend):
                lax.fori_loop(0, heads // 2, attend, 0)

        send_a = remote(a_out, a_in.at[c], a_s.at[0], a_r.at[c], d1)
        send_b = remote(b_out, b_in.at[c], b_s.at[0], b_r.at[c], d1)
        send_x = remote(x_out.at[c], x_in.at[c], x_s.at[c], x_r.at[c], d2)

        @pl.when(c == 0)
        def _():
            for r in (3, 1, 2):
                wo_copies[r].wait()

        @pl.when(c > 0)
        def _():
            send_a.wait_send()
            send_b.wait_send()

        def project(r, n):
            cols = pl.ds(pl.multiple_of(n * 512, 512), 512)
            return cols, jnp.dot(ctx[here, :], wo[r, :, cols], preferred_element_type=F32)

        def part_a(n, carry):
            cols, t = project(3, n)
            a_out[:, cols] = t.astype(BF16)
            return carry

        lax.fori_loop(0, width // 512, part_a, 0)
        send_a.start()

        def part_b(n, carry):
            cols, t = project(1, n)
            b_out[:, cols] = t.astype(BF16)
            return carry

        lax.fori_loop(0, width // 512, part_b, 0)
        send_b.start()
        send_a.wait_recv()

        def part_x(n, carry):
            cols, t = project(2, n)
            x_out[c, :, cols] = (t + a_in[c, :, cols].astype(F32)).astype(BF16)
            return carry

        lax.fori_loop(0, width // 512, part_x, 0)
        send_x.start()
        return carry

    lax.fori_loop(0, CHUNKS, chunk, 0)
    wo_copies[0].wait()

    def prepare(c):
        remote(b_out, b_in.at[c], b_s.at[0], b_r.at[c], d1).wait_recv()

        def own(n, carry):
            cols = pl.ds(pl.multiple_of(n * 256, 256), 256)
            t = jnp.dot(ctx[rows_of(c), :], wo[0, :, cols], preferred_element_type=F32)
            t = t + b_in[c, :, cols].astype(F32) + out[rows_of(c), cols].astype(F32)
            kvp[(c % 2) * 2 + n // 4, pl.ds(pl.multiple_of((n % 4) * R, R), R), :] = t
            return carry

        lax.fori_loop(0, width // 256, own, 0)

    kv_a.wait_send()
    kv_b.wait_send()
    prepare(0)

    def finish(c, carry):
        @pl.when(c + 1 < CHUNKS)
        def _():
            prepare(c + 1)

        remote(x_out.at[c], x_in.at[c], x_s.at[c], x_r.at[c], d2).wait_recv()
        for n in range(width // 256):
            cols = slice(n * 256, (n + 1) * 256)
            t = kvp[(c % 2) * 2 + n // 4, (n % 4) * R : (n % 4 + 1) * R, :]
            out[rows_of(c), cols] = (t + x_in[c, :, cols].astype(F32)).astype(BF16)
        return carry

    lax.fori_loop(0, CHUNKS, finish, 0)

    kv_x.wait_send()
    remote(a_out, a_in.at[0], a_s.at[0], a_r.at[0], d1).wait_send()
    remote(b_out, b_in.at[0], b_s.at[0], b_r.at[0], d1).wait_send()
    for c in range(CHUNKS):
        gather_x(c).wait_send()
        gather_core(c).wait_send()
        forward(c).wait_send()
        remote(x_out.at[c], x_in.at[c], x_s.at[c], x_r.at[c], d2).wait_send()


def fused(hidden_in, norm_gain, w_query, w_keyval, w_out, hyp_ids):
    rows, width = hidden_in.shape
    R = rows // CHUNKS
    qc = w_query.shape[1]
    exponent = np.arange(HD // 2, dtype=np.float32) * np.float32(2.0 / HD)
    base = np.power(np.float32(500000.0), -exponent).astype(np.float32)
    freq = jnp.asarray(np.concatenate([base, base])[None, :])
    vmem = pl.BlockSpec(memory_space=pltpu.VMEM)
    hbm = pl.BlockSpec(memory_space=pl.ANY)
    dma = pltpu.SemaphoreType.DMA
    return pl.pallas_call(
        kernel,
        out_shape=pltpu.VMEM((rows, width), BF16),
        in_specs=[hbm] * 7,
        out_specs=vmem,
        scratch_shapes=[
            pltpu.VMEM((1, 4 * width), F32),
            pltpu.VMEM((1, HD), F32),
            pltpu.VMEM((1, rows), jnp.int32),
            pltpu.VMEM((3, rows, width), BF16),
            pltpu.VMEM((4, width, qc), BF16),
            pltpu.VMEM((4, qc, width), BF16),
            pltpu.VMEM((4, R, width), BF16),
            pltpu.VMEM((4, rows, 2 * HD), F32),
            pltpu.VMEM((2, rows, 2 * HD), F32),
            pltpu.VMEM((rows, 2 * HD), BF16),
            pltpu.VMEM((rows, 2 * HD), BF16),
            pltpu.VMEM((rows, HD), BF16),
            pltpu.VMEM((rows, HD), BF16),
            pltpu.VMEM((R, qc), BF16),
            pltpu.VMEM((rows, qc), BF16),
            pltpu.VMEM((R, width), BF16),
            pltpu.VMEM((R, width), BF16),
            pltpu.VMEM((CHUNKS, R, width), BF16),
            pltpu.VMEM((CHUNKS, R, width), BF16),
            pltpu.VMEM((CHUNKS, R, width), BF16),
            pltpu.VMEM((CHUNKS, R, width), BF16),
            dma((CHUNKS,)), dma((CHUNKS,)), dma((CHUNKS,)),
            dma((CHUNKS,)), dma((CHUNKS,)), dma((CHUNKS,)),
            dma((3,)), dma((3,)),
            dma((1,)), dma((1,)), dma((CHUNKS,)),
            dma((CHUNKS,)), dma((CHUNKS,)), dma((CHUNKS,)),
            dma((3,)), dma((1,)), dma((16,)), dma((4,)), dma((4,)),
        ],
        compiler_params=pltpu.CompilerParams(
            collective_id=0, has_side_effects=True, vmem_limit_bytes=VMEM_LIMIT
        ),
    )(
        hidden_in, norm_gain.reshape(1, -1), freq, hyp_ids.reshape(1, -1),
        w_query, w_keyval, w_out,
    )


VMEM_LIMIT = 60 * 1024 * 1024


def positions(ids):
    rows = ids.shape[0]
    row = jnp.arange(rows, dtype=jnp.int32)
    prev = jnp.concatenate([jnp.full((1,), -2, jnp.int32), ids[:-1]])
    start = jnp.where(ids != prev, row, jnp.zeros_like(row))
    start = lax.cummax(start, axis=0)
    return (row - start).astype(jnp.float32)


def rotate(heads, pos):
    half = heads.shape[-1] // 2
    freq = 500000.0 ** (-jnp.arange(half, dtype=jnp.float32) * 2.0 / heads.shape[-1])
    angle = pos[:, None] * freq[None, :]
    cosine = jnp.cos(angle)[:, None, :]
    sine = jnp.sin(angle)[:, None, :]
    first = heads[..., :half]
    second = heads[..., half:]
    return jnp.concatenate(
        [first * cosine - second * sine, second * cosine + first * sine], axis=-1
    )


def shards(hidden_in, norm_gain, w_query, w_keyval, w_out, hyp_ids):
    rows = hidden_in.shape[0]
    local_width = hidden_in.shape[1]
    shard = lax.axis_index("tensor")
    local_gain = lax.dynamic_slice_in_dim(norm_gain, shard * local_width, local_width)
    local_normed = (hidden_in.astype(jnp.float32) * local_gain[None, :]).astype(jnp.bfloat16)
    kv_term = jnp.dot(local_normed, w_keyval, preferred_element_type=jnp.float32)
    keyval = lax.psum(kv_term, "tensor")
    whole = lax.all_gather(hidden_in, "tensor", axis=1, tiled=True)
    wide = whole.astype(jnp.float32)
    squares = jnp.sum(wide * wide, axis=-1)
    normed = (wide * norm_gain[None, :]).astype(jnp.bfloat16)
    query_raw = jnp.dot(normed, w_query, preferred_element_type=jnp.float32)
    scale = lax.rsqrt(squares / D + 1e-05)
    pos = positions(hyp_ids)
    local_heads = w_query.shape[1] // HD
    query = rotate((query_raw * scale[:, None]).reshape(rows, local_heads, HD), pos).astype(
        jnp.bfloat16
    )
    keyval = keyval * scale[:, None]
    keys = rotate(keyval[:, : KVH * HD].reshape(rows, KVH, HD), pos)
    values = keyval[:, KVH * HD :].reshape(rows, KVH, HD)
    group = HEADS // KVH
    head_index = shard * local_heads + jnp.arange(local_heads, dtype=jnp.int32)
    select = (head_index[:, None] // group == jnp.arange(KVH, dtype=jnp.int32)[None, :]).astype(
        jnp.float32
    )
    keys = jnp.einsum("tgd,hg->thd", keys.astype(jnp.bfloat16).astype(jnp.float32), select).astype(
        jnp.bfloat16
    )
    values = jnp.einsum(
        "tgd,hg->thd", values.astype(jnp.bfloat16).astype(jnp.float32), select
    ).astype(jnp.bfloat16)
    row = jnp.arange(rows, dtype=jnp.int32)
    allowed = (
        (hyp_ids[:, None] == hyp_ids[None, :])
        & (hyp_ids[:, None] >= 0)
        & (row[None, :] <= row[:, None])
    )
    scores = jnp.einsum("qhd,khd->hqk", query, keys, preferred_element_type=jnp.float32) / jnp.sqrt(
        jnp.float32(HD)
    )
    scores = jnp.where(allowed[None], scores, jnp.float32(-1e30))
    peak = jnp.max(scores, axis=-1, keepdims=True)
    expo = jnp.where(allowed[None], jnp.exp(scores - peak), jnp.float32(0.0))
    total = jnp.maximum(jnp.sum(expo, axis=-1, keepdims=True), 1.0)
    probs = (expo / total).astype(jnp.bfloat16)
    context = jnp.einsum("hqk,khd->qhd", probs, values, preferred_element_type=jnp.float32)
    context = context.astype(jnp.bfloat16).reshape(rows, local_heads * HD)
    out_term = jnp.dot(context, w_out, preferred_element_type=jnp.float32)
    summed = lax.psum_scatter(out_term, "tensor", scatter_dimension=1, tiled=True)
    return (hidden_in.astype(jnp.float32) + summed).astype(jnp.bfloat16)


def solution(mesh):
    body = fused if mesh.shape["tensor"] == 4 else shards
    return jax.shard_map(
        body,
        mesh=mesh,
        in_specs=(
            P(("groups", "dp"), "tensor"),
            P(),
            P(None, "tensor"),
            P("tensor", None),
            P("tensor", None),
            P(("groups", "dp")),
        ),
        out_specs=P(("groups", "dp"), "tensor"),
        check_vma=False,
    )
```
